768 devices in a mesh: cuts: 16 (over y_hi, x, core), fsdp: 4 (over y_lo), tensor: 12 (over z).
Axes of the slice: x: 4, y: 8 (y_hi: 2, y_lo: 4; y = y_hi * 4 + y_lo), z: 12, core: 2. Of those that a mesh axis runs over, the one named last changes fastest.
Arguments:
- attn_out: bfloat16 [24576, 4608], P(('cuts', 'fsdp'), 'tensor'), may hold values from -6 to 6
- grad_out: bfloat16 [24576, 4096], P(('cuts', 'fsdp', 'tensor')), may hold values from -6 to 6
- weight: bfloat16 [4096, 4608], P('fsdp', 'tensor'), may hold values from -0.09375 to 0.09375
- master: float32 [4096, 4608], P(('fsdp', 'cuts'), 'tensor'), may hold values from -0.3 to 0.3
- moment: float32 [4096, 4608], P(('fsdp', 'cuts'), 'tensor'), may hold values from -6 to 6
- second: float32 [4096, 4608], P(('fsdp', 'cuts'), 'tensor'), may hold values from 0.25 to 4
Outputs:
- grad_input: bfloat16 [24576, 4608], P(('cuts', 'fsdp'), 'tensor')
- fresh_weight: bfloat16 [4096, 4608], P('fsdp', 'tensor')
- master_new: float32 [4096, 4608], P(('fsdp', 'cuts'), 'tensor')
- moment_new: float32 [4096, 4608], P(('fsdp', 'cuts'), 'tensor')
- second_new: float32 [4096, 4608], P(('fsdp', 'cuts'), 'tensor')
The draws below stay inside these ranges and needn't reach their ends.
All inputs are finite; a program needn't handle non-finite values.
Results may differ from the reference program's by a relative error of at most 0.0034.
Values may be sent and summed in bfloat16 or wider, within the bound.
A program may use at most 64 MiB of HBM per device.

```python
import math
import jax
import jax.numpy as jnp
from jax import lax

HID = 4608
DOUT = 4096
GROUP_ROWS = 384
TOKENS = 24576


def steps_of(rng, extent, shards, low, top_value):
    def one(position, parts):
        heights = jax.random.uniform(jax.random.fold_in(jax.random.fold_in(rng, 6), position), (parts,), jnp.float32, low / len(shards), top_value / len(shards))
        return jnp.repeat(jnp.exp(heights), extent[position] // parts).reshape((-1,) + (1,) * (len(extent) - position - 1))

    loudness = one(*shards[0])
    for cut in shards[1:]:
        loudness = loudness * one(*cut)
    return loudness


def normal_values(key, shape, scale, limit, split=(), held_as=jnp.bfloat16):
    array = jax.random.normal(key, shape, jnp.float32) * scale
    if len(split) > 0:
        array = steps_of(key, shape, split, -0.22, 0.18) * array
    return jnp.clip(array, min=-limit, max=limit).astype(held_as)


def setup_inputs(seed: int = 0) -> dict:
    streams_of = jax.random.split(jax.random.key(seed), 7)
    attn_out = normal_values(streams_of[0], (TOKENS, HID), 1.0, 6.0, ((0, 64), (1, 12)))
    grad_out = normal_values(streams_of[1], (TOKENS, DOUT), 1.0, 6.0, ((0, 768),))
    weight = normal_values(streams_of[2], (DOUT, HID), DOUT ** -0.5, 0.09375, ((0, 4), (1, 12)))
    master = normal_values(streams_of[3], (DOUT, HID), 0.05, 0.3, ((0, 64), (1, 12)), jnp.float32)
    moment = normal_values(streams_of[4], (DOUT, HID), 1.0, 6.0, ((0, 64), (1, 12)), jnp.float32)
    second = jnp.clip(jnp.exp(math.log(4.0) - 2.7725887 * jax.random.uniform(streams_of[5], (DOUT, HID), jnp.float32) ** steps_of(streams_of[5], (DOUT, HID), ((0, 64), (1, 12)), -0.2, 0.2)), 0.25, 4.0)
    return {"attn_out": attn_out, "grad_out": grad_out, "weight": weight, "master": master, "moment": moment, "second": second}


def reference(attn_out, grad_out, weight, master, moment, second):
    grad_input = jnp.dot(grad_out.astype(jnp.float32), weight.astype(jnp.float32)).astype(jnp.bfloat16)
    group_count = TOKENS // GROUP_ROWS
    x_groups = attn_out.reshape(group_count, GROUP_ROWS, HID)
    g_groups = grad_out.reshape(group_count, GROUP_ROWS, DOUT)

    def accumulate(running, group_pair):
        x_rows, g_rows = group_pair
        partial_value = jnp.dot(g_rows.astype(jnp.float32).T, x_rows.astype(jnp.float32))
        rounded = lax.optimization_barrier(partial_value.astype(jnp.bfloat16))
        return (running + rounded.astype(jnp.float32), None)
    summed, unused = lax.scan(accumulate, jnp.zeros((DOUT, HID), jnp.float32), (x_groups, g_groups))
    gradient = summed * (1.0 / math.sqrt(TOKENS))
    moment_new = 0.9 * moment + 0.1 * gradient
    second_new = 0.95 * second + 0.05 * gradient * gradient
    adam_step = moment_new / (1.0 - 0.9 ** 10) / (jnp.sqrt(second_new / (1.0 - 0.95 ** 10)) + 1e-08)
    master_new = master - 0.02 * (adam_step + 0.1 * master)
    return (grad_input, master_new.astype(jnp.bfloat16), master_new, moment_new, second_new)
```

```python
import functools
import math

import jax
import jax.numpy as jnp
from jax import lax
from jax.experimental import pallas as pl
from jax.experimental.pallas import tpu as pltpu
from jax.sharding import PartitionSpec as P

BF16 = jnp.bfloat16
F32 = jnp.float32
NX, NY, NF = 4, 8, 4
CHUNKS = NY


def kernel(
    nz,
    scale,
    attn,
    gout,
    weight,
    master,
    moment,
    second,
    gi_out,
    fresh,
    master_new,
    moment_new,
    second_new,
    gbuf,
    abuf,
    wbuf,
    pbuf,
    rbuf,
    sbuf,
    ybuf,
    acc,
    gibuf,
    mst,
    mom,
    sec,
    zs,
    zr,
    cs,
    cr,
    cl,
    asend,
    arecv,
    aloc,
    ws,
    wr,
    wl,
    xs,
    xr,
    ys,
    yr,
    fs,
    fr,
    gs,
    gr,
    ol,
):
    cuts = lax.axis_index("cuts")
    f = lax.axis_index("fsdp")
    z = lax.axis_index("tensor")
    core = lax.rem(cuts, 2)
    x = lax.rem(lax.div(cuts, 2), NX)
    yh = lax.div(cuts, 2 * NX)
    y = yh * NF + f
    rows = gout.shape[0]
    half = 256
    group = rows * nz

    def dev(px, py, pcore, pz):
        return {
            "cuts": lax.div(py, NF) * (2 * NX) + px * 2 + pcore,
            "fsdp": lax.rem(py, NF),
            "tensor": pz,
        }

    def remote(src, dst, send, recv, target):
        return pltpu.make_async_remote_copy(
            src_ref=src,
            dst_ref=dst,
            send_sem=send,
            recv_sem=recv,
            device_id=target,
            device_id_type=pl.DeviceIdType.MESH,
        )

    sibling = dev(x, y, 1 - core, z)
    z_next = dev(x, y, core, lax.rem(z + 1, nz))
    z_prev = dev(x, y, core, lax.rem(z + nz - 1, nz))
    y_next = dev(x, lax.rem(y + 1, NY), core, z)
    y_prev = dev(x, lax.rem(y + NY - 1, NY), core, z)

    own_state = [
        pltpu.make_async_copy(src, dst, ol.at[i])
        for i, (src, dst) in enumerate(((master, mst), (moment, mom), (second, sec)))
    ]
    attn_local = pltpu.make_async_copy(attn, abuf.at[core], aloc.at[0])

    def dest_y(s):
        sign = 1 - 2 * lax.rem(s, 2)
        return lax.rem(y + NF + sign * lax.div(s + 1, 2), NY)

    def columns(s, of_core):
        to = dest_y(s)
        q = lax.rem(to, NF) * 2 + lax.div(to, NF)
        return pl.ds(pl.multiple_of(q * 512 + of_core * half, half), half)

    def own_chunk(s):
        return pltpu.make_async_copy(
            gout.at[:, columns(s, core)], gbuf.at[s, core, z], cl.at[s]
        )

    def core_chunk(s, me):
        return remote(
            gout.at[:, columns(s, 1 - me)], gbuf.at[s, me, z], cs.at[s], cr.at[s], sibling
        )

    def weight_rows(i):
        return pl.ds(pl.multiple_of(i * 512 + core * half, half), half)

    def weight_local(i):
        return pltpu.make_async_copy(
            weight.at[weight_rows(i)], wbuf.at[f + NF * i], wl.at[i]
        )

    f_up, f_down = lax.rem(f + 1, NF), lax.rem(f + NF - 1, NF)

    def weight_to_prev(i):
        return remote(
            weight.at[weight_rows(i)], wbuf.at[f + NF * i], ws.at[i], wr.at[i], y_prev
        )

    def weight_to_next(i):
        return remote(
            weight.at[weight_rows(i)], wbuf.at[f + NF * i], ws.at[2 + i], wr.at[2 + i], y_next
        )

    def weight_pass_prev():
        return remote(wbuf.at[f_up], wbuf.at[f_up], ws.at[4], wr.at[4], y_prev)

    def weight_pass_next():
        return remote(wbuf.at[f_down + NF], wbuf.at[f_down + NF], ws.at[5], wr.at[5], y_next)

    def z_copy(d, s, h):
        if d == 0:
            block = lax.rem(z - h + nz, nz)
            target = z_next
        else:
            block = lax.rem(z + h, nz)
            target = z_prev
        ref = gbuf.at[s, :, block]
        return remote(ref, ref, zs.at[d, s, h], zr.at[d, s, h], target)

    def z_arrived(d, s, h):
        if d == 0:
            block = lax.rem(z - 1 - h + nz, nz)
            target = z_next
        else:
            block = lax.rem(z + 1 + h, nz)
            target = z_prev
        ref = gbuf.at[s, :, block]
        return remote(ref, ref, zs.at[d, s, h], zr.at[d, s, h], target)

    def x_half(s, j, b):
        px = 2 * core + j
        src = pbuf.at[s, pl.ds(j * 128 + b * 64, 64)]
        return px, src, rbuf.at[s, x], j * 2 + b

    def x_self(px, b):
        return jnp.logical_and(px == x, core == b)

    def x_start(s):
        for j in range(2):
            for b in range(2):
                px, src, dst, k = x_half(s, j, b)
                here = x_self(px, b)

                @pl.when(here)
                def _():
                    pltpu.make_async_copy(src, dst, xr.at[s, x]).start()

                @pl.when(jnp.logical_not(here))
                def _():
                    remote(src, dst, xs.at[s, k], xr.at[s, x], dev(px, y, b, z)).start()

    def x_sent(s):
        for j in range(2):
            for b in range(2):
                px, src, dst, k = x_half(s, j, b)

                @pl.when(jnp.logical_not(x_self(px, b)))
                def _():
                    remote(src, dst, xs.at[s, k], xr.at[s, x], dev(px, y, b, z)).wait_send()

    def x_arrived(s):
        for i in range(NX):
            remote(
                pbuf.at[s, pl.ds(0, 64)], rbuf.at[s, i], xs.at[s, 0], xr.at[s, i], sibling
            ).wait_recv()

    def y_copy(s):
        return remote(
            sbuf.at[s], ybuf.at[s], ys.at[s], yr.at[s], dev(x, dest_y(s), core, z)
        )

    def piece(py_hi, px, pcore):
        at = (py_hi * (2 * NX) + px * 2 + pcore) * 64
        return fresh.at[pl.ds(pl.multiple_of(at, 64), 64)]

    partner = dev(x, lax.rem(y + NF, NY), core, z)

    def fresh_copy(i, src, target):
        return remote(src, src, fs.at[i], fr.at[i], target)

    for copy in own_state:
        copy.start()
    attn_local.start()
    for i in range(2):
        weight_local(i).start()

    def start_own(s, carry):
        own_chunk(s).start()
        return carry

    lax.fori_loop(0, CHUNKS, start_own, 0)

    barrier = pltpu.get_barrier_semaphore()
    peers = [sibling, z_next, z_prev]
    for i in range(1, NY):
        peers.append(dev(x, lax.rem(y + i, NY), core, z))
    for i in range(1, NX):
        for b in range(2):
            peers.append(dev(lax.rem(x + i, NX), y, b, z))
    for peer in peers:
        pl.semaphore_signal(
            barrier, inc=1, device_id=peer, device_id_type=pl.DeviceIdType.MESH
        )
    pl.semaphore_wait(barrier, len(peers))

    def start_core(s, carry):
        core_chunk(s, core).start()
        return carry

    lax.fori_loop(0, CHUNKS, start_core, 0)
    attn_remote = remote(attn, abuf.at[core], asend.at[0], arecv.at[0], sibling)
    attn_remote.start()
    for i in range(2):
        weight_to_prev(i).start()
        weight_to_next(1 - i).start()
    acc[...] = jnp.zeros_like(acc)
    for i in range(2):
        weight_local(i).wait()

    def forward(s, h):
        if h == 0:
            own_chunk(s).wait()
            core_chunk(s, 1 - core).wait_recv()
        for d in range(2):

            def go():
                if h > 0:
                    z_arrived(d, s, h - 1).wait_recv()
                z_copy(d, s, h).start()

            if h < 5:
                go()
            else:
                pl.when(lax.rem(s, 2) == d)(go)

    def gathered(s):
        for d in range(2):

            @pl.when(lax.rem(s, 2) == d)
            def _():
                z_arrived(d, s, 5).wait_recv()
                z_arrived(1 - d, s, 4).wait_recv()

    def when_chunk(s, go):
        @pl.when(jnp.logical_and(s >= 0, s < CHUNKS))
        def _():
            go(jnp.clip(s, 0, CHUNKS - 1))

    def weight_gradient(s):
        gathered(s)
        g = gbuf[s].reshape(2 * group, half)
        a = abuf[...].reshape(2 * group, abuf.shape[-1])
        part = lax.dot_general(g, a, (((0,), (0,)), ((), ())), preferred_element_type=F32)
        pbuf[s] = part.astype(BF16)
        x_start(s)

    def input_gradient(s):
        g = gbuf[s].reshape(2 * group, half)
        acc[...] += jnp.dot(g, wbuf[dest_y(s)], preferred_element_type=F32)

    def row_sum(s):
        x_arrived(s)
        total = rbuf[s, 0].astype(F32)
        for i in range(1, NX):
            total = total + rbuf[s, i].astype(F32)
        return total

    def to_owner(s):
        sbuf[s] = row_sum(s).astype(BF16)
        y_copy(s).start()

    def step(u, carry):
        when_chunk(u - 2, lambda s: forward(s, 4))
        when_chunk(u - 1, lambda s: forward(s, 2))
        when_chunk(u, lambda s: forward(s, 0))

        @pl.when(u == 2)
        def _():
            remote(wbuf.at[f_up], wbuf.at[f_up], ws.at[0], wr.at[0], y_prev).wait_recv()
            weight_pass_prev().start()
            down = wbuf.at[f_down + NF]
            remote(down, down, ws.at[3], wr.at[3], y_next).wait_recv()
            weight_pass_next().start()

        @pl.when(u == 3)
        def _():
            attn_local.wait()
            remote(attn, abuf.at[1 - core], asend.at[0], arecv.at[0], sibling).wait_recv()

        @pl.when(u == 4)
        def _():
            up = wbuf.at[f_up + NF]
            remote(up, up, ws.at[1], wr.at[1], y_prev).wait_recv()
            down = wbuf.at[f_down]
            remote(down, down, ws.at[2], wr.at[2], y_next).wait_recv()

        @pl.when(u == 6)
        def _():
            far = lax.rem(f + 2, NF)
            remote(wbuf.at[far], wbuf.at[far], ws.at[4], wr.at[4], y_prev).wait_recv()
            far_hi = wbuf.at[far + NF]
            remote(far_hi, far_hi, ws.at[5], wr.at[5], y_next).wait_recv()

        when_chunk(u - 3, weight_gradient)
        when_chunk(u - 2, lambda s: forward(s, 5))
        when_chunk(u - 1, lambda s: forward(s, 3))
        when_chunk(u, lambda s: forward(s, 1))

        @pl.when(u >= 4)
        def _():
            to_owner(u - 4)

        when_chunk(u - 3, input_gradient)
        return carry

    lax.fori_loop(0, CHUNKS + 3, step, 0)

    gi_copy = remote(acc.at[pl.ds((1 - core) * group, group)], gibuf, gs.at[0], gr.at[0], sibling)
    gi_copy.start()

    summed = row_sum(CHUNKS - 1)
    for s in range(CHUNKS - 1):
        y_copy(s).wait_recv()
        summed = summed + ybuf[s].astype(F32)
    for copy in own_state:
        copy.wait()
    gradient = summed * scale
    moment_next = 0.9 * mom[...] + 0.1 * gradient
    second_next = 0.95 * sec[...] + 0.05 * gradient * gradient
    adam_step = (
        moment_next / (1.0 - 0.9**10) / (jnp.sqrt(second_next / (1.0 - 0.95**10)) + 1e-08)
    )
    master_next = mst[...] - 0.02 * (adam_step + 0.1 * mst[...])
    mine = piece(yh, x, core)
    mine[...] = master_next.astype(BF16)

    sent = []

    def send(i, ref, target):
        copy = fresh_copy(i, ref, target)
        copy.start()
        sent.append(copy)

    def x_peer(i):
        return dev(lax.rem(x + i, NX), y, core, z)

    send(0, mine, partner)
    for i in (2, 1, 3):
        send(i, mine, x_peer(i))
    send(4, mine, sibling)
    moment_new[...] = moment_next
    second_new[...] = second_next
    master_new[...] = master_next

    far = piece(1 - yh, x, core)
    fresh_copy(0, far, sibling).wait_recv()
    for i in (2, 1, 3):
        send(4 + i, far, x_peer(i))
    send(8, far, sibling)
    gi_copy.wait_recv()
    mine_rows = pl.ds(pl.multiple_of(core * group, group), group)
    gi_out[...] = (acc[mine_rows] + gibuf[...]).astype(BF16)
    for hi, base in ((yh, 0), (1 - yh, 4)):
        for i in (1, 3, 2):
            got = piece(hi, lax.rem(x - i + NX, NX), core)
            fresh_copy(base + i, got, sibling).wait_recv()
            send(8 + base + i if base == 0 else 8 + 3 + i, got, sibling)
    other = 1 - core
    fresh_copy(4, piece(yh, x, other), sibling).wait_recv()
    fresh_copy(8, piece(1 - yh, x, other), sibling).wait_recv()
    for hi, base in ((yh, 8), (1 - yh, 11)):
        for i in (1, 3, 2):
            got = piece(hi, lax.rem(x - i + NX, NX), other)
            fresh_copy(base + i, got, sibling).wait_recv()

    def sent_chunk(s, carry):
        core_chunk(s, core).wait_send()
        for d in range(2):
            for h in range(5):
                z_copy(d, s, h).wait_send()

            @pl.when(lax.rem(s, 2) == d)
            def _():
                z_copy(d, s, 5).wait_send()

        x_sent(s)

        @pl.when(s < CHUNKS - 1)
        def _():
            y_copy(s).wait_send()

        return carry

    lax.fori_loop(0, CHUNKS, sent_chunk, 0)
    attn_remote.wait_send()
    for i in range(2):
        weight_to_prev(i).wait_send()
        weight_to_next(i).wait_send()
    weight_pass_prev().wait_send()
    weight_pass_next().wait_send()
    gi_copy.wait_send()
    for copy in sent:
        copy.wait_send()


def shards(attn_out, grad_out, weight, master, moment, second):
    nz = lax.axis_size("tensor")
    rows, dout = grad_out.shape
    group, hid = attn_out.shape
    half = dout // (2 * CHUNKS)
    state_rows = master.shape[0]
    total_tokens = rows * lax.axis_size("cuts") * lax.axis_size("fsdp") * nz
    dma = pltpu.SemaphoreType.DMA
    any_spec = pl.BlockSpec(memory_space=pl.ANY)
    vmem_spec = pl.BlockSpec(memory_space=pltpu.VMEM)
    state = jax.ShapeDtypeStruct(master.shape, F32)
    return pl.pallas_call(
        functools.partial(kernel, nz, 1.0 / math.sqrt(total_tokens)),
        out_shape=(
            jax.ShapeDtypeStruct((group, hid), BF16),
            jax.ShapeDtypeStruct(weight.shape, BF16),
            state,
            state,
            state,
        ),
        in_specs=[any_spec] * 6,
        out_specs=(vmem_spec,) * 5,
        scratch_shapes=[
            pltpu.VMEM((CHUNKS, 2, nz, rows, half), BF16),
            pltpu.VMEM((2, group, hid), BF16),
            pltpu.VMEM((CHUNKS, half, hid), BF16),
            pltpu.VMEM((CHUNKS, half, hid), BF16),
            pltpu.VMEM((CHUNKS, NX, state_rows, hid), BF16),
            pltpu.VMEM((CHUNKS, state_rows, hid), BF16),
            pltpu.VMEM((CHUNKS, state_rows, hid), BF16),
            pltpu.VMEM((2 * group, hid), F32),
            pltpu.VMEM((group, hid), F32),
            pltpu.VMEM((state_rows, hid), F32),
            pltpu.VMEM((state_rows, hid), F32),
            pltpu.VMEM((state_rows, hid), F32),
            dma((2, CHUNKS, 6)),
            dma((2, CHUNKS, 6)),
            dma((CHUNKS,)),
            dma((CHUNKS,)),
            dma((CHUNKS,)),
            dma((1,)),
            dma((1,)),
            dma((1,)),
            dma((6,)),
            dma((6,)),
            dma((2,)),
            dma((CHUNKS, 4)),
            dma((CHUNKS, NX)),
            dma((CHUNKS,)),
            dma((CHUNKS,)),
            dma((16,)),
            dma((16,)),
            dma((1,)),
            dma((1,)),
            dma((3,)),
        ],
        compiler_params=pltpu.CompilerParams(
            collective_id=0, has_side_effects=True, vmem_limit_bytes=48 * 1024 * 1024
        ),
    )(attn_out, grad_out, weight, master, moment, second)


def solution(mesh):
    return jax.shard_map(
        shards,
        mesh=mesh,
        in_specs=(
            P(("cuts", "fsdp"), "tensor"),
            P(("cuts", "fsdp", "tensor"), None),
            P("fsdp", "tensor"),
            P(("fsdp", "cuts"), "tensor"),
            P(("fsdp", "cuts"), "tensor"),
            P(("fsdp", "cuts"), "tensor"),
        ),
        out_specs=(
            P(("cuts", "fsdp"), "tensor"),
            P("fsdp", "tensor"),
            P(("fsdp", "cuts"), "tensor"),
            P(("fsdp", "cuts"), "tensor"),
            P(("fsdp", "cuts"), "tensor"),
        ),
        check_vma=False,
    )
```

```python
import functools
import math

import jax
import jax.numpy as jnp
from jax import lax
from jax.experimental import pallas as pl
from jax.experimental.pallas import tpu as pltpu
from jax.sharding import PartitionSpec as P

BF16 = jnp.bfloat16
F32 = jnp.float32
NX, NY, NF = 4, 8, 4
CHUNKS = NY
STARTS = (0, 0, 0, 1, 1, 2, 2, 3)
VMEM_LIMIT = 60 * 1024 * 1024


def kernel(
    nz,
    scale,
    attn,
    gout,
    weight,
    master,
    moment,
    second,
    gi_out,
    fresh,
    master_new,
    moment_new,
    second_new,
    gbuf,
    abuf,
    wbuf,
    pbuf,
    rbuf,
    sbuf,
    ybuf,
    acc,
    gibuf,
    mst,
    mom,
    sec,
    zs,
    zr,
    cs,
    cr,
    cl,
    asend,
    arecv,
    aloc,
    ws,
    wr,
    wl,
    xs,
    xr,
    ys,
    yr,
    fs,
    fr,
    gs,
    gr,
    ol,
):
    cuts = lax.axis_index("cuts")
    f = lax.axis_index("fsdp")
    z = lax.axis_index("tensor")
    core = lax.rem(cuts, 2)
    x = lax.rem(lax.div(cuts, 2), NX)
    yh = lax.div(cuts, 2 * NX)
    y = yh * NF + f
    rows = gout.shape[0]
    half = 256
    group = rows * nz

    def dev(px, py, pcore, pz):
        return {
            "cuts": lax.div(py, NF) * (2 * NX) + px * 2 + pcore,
            "fsdp": lax.rem(py, NF),
            "tensor": pz,
        }

    def remote(src, dst, send, recv, target):
        return pltpu.make_async_remote_copy(
            src_ref=src,
            dst_ref=dst,
            send_sem=send,
            recv_sem=recv,
            device_id=target,
            device_id_type=pl.DeviceIdType.MESH,
        )

    sibling = dev(x, y, 1 - core, z)
    z_next = dev(x, y, core, lax.rem(z + 1, nz))
    z_prev = dev(x, y, core, lax.rem(z + nz - 1, nz))
    y_next = dev(x, lax.rem(y + 1, NY), core, z)
    y_prev = dev(x, lax.rem(y + NY - 1, NY), core, z)

    own_state = [
        pltpu.make_async_copy(src, dst, ol.at[i])
        for i, (src, dst) in enumerate(((master, mst), (moment, mom), (second, sec)))
    ]
    attn_local = pltpu.make_async_copy(attn, abuf.at[core], aloc.at[0])

    row_of = [lax.rem(y + NF + (1 - 2 * (s % 2)) * ((s + 1) // 2), NY) for s in range(CHUNKS)]
    row_dev = [dev(x, row, core, z) for row in row_of]
    z_of = [lax.rem(z + i, nz) for i in range(nz)]

    def columns(s, of_core):
        to = row_of[s]
        q = lax.rem(to, NF) * 2 + lax.div(to, NF)
        return pl.ds(pl.multiple_of(q * 512 + of_core * half, half), half)

    def own_chunk(s):
        return pltpu.make_async_copy(
            gout.at[:, columns(s, core)], gbuf.at[s, core, z], cl.at[s]
        )

    def core_chunk(s, me):
        return remote(
            gout.at[:, columns(s, 1 - me)], gbuf.at[s, me, z], cs.at[s], cr.at[s], sibling
        )

    def weight_rows(i):
        return pl.ds(pl.multiple_of(i * 512 + core * half, half), half)

    def weight_local(i):
        return pltpu.make_async_copy(
            weight.at[weight_rows(i)], wbuf.at[f + NF * i], wl.at[i]
        )

    f_up, f_down = lax.rem(f + 1, NF), lax.rem(f + NF - 1, NF)

    def weight_to_prev(i):
        return remote(
            weight.at[weight_rows(i)], wbuf.at[f + NF * i], ws.at[i], wr.at[i], y_prev
        )

    def weight_to_next(i):
        return remote(
            weight.at[weight_rows(i)], wbuf.at[f + NF * i], ws.at[2 + i], wr.at[2 + i], y_next
        )

    def weight_pass_prev():
        return remote(wbuf.at[f_up], wbuf.at[f_up], ws.at[4], wr.at[4], y_prev)

    def weight_pass_next():
        return remote(wbuf.at[f_down + NF], wbuf.at[f_down + NF], ws.at[5], wr.at[5], y_next)

    def z_copy(d, s, h):
        if d == 0:
            block = z_of[-h % nz]
            target = z_next
        else:
            block = z_of[h]
            target = z_prev
        ref = gbuf.at[s, :, block]
        return remote(ref, ref, zs.at[d, s, h], zr.at[d, s, h], target)

    def z_arrived(d, s, h):
        if d == 0:
            block = z_of[(-1 - h) % nz]
            target = z_next
        else:
            block = z_of[1 + h]
            target = z_prev
        ref = gbuf.at[s, :, block]
        return remote(ref, ref, zs.at[d, s, h], zr.at[d, s, h], target)

    def x_half(s, j, b):
        px = 2 * core + j
        src = pbuf.at[s, pl.ds(j * 128 + b * 64, 64)]
        return px, src, rbuf.at[s, x], j * 2 + b

    def x_self(px, b):
        return jnp.logical_and(px == x, core == b)

    def x_start(s):
        for j in range(2):
            for b in range(2):
                px, src, dst, k = x_half(s, j, b)
                here = x_self(px, b)

                @pl.when(here)
                def _():
                    pltpu.make_async_copy(src, dst, xr.at[s, x]).start()

                @pl.when(jnp.logical_not(here))
                def _():
                    remote(src, dst, xs.at[s, k], xr.at[s, x], dev(px, y, b, z)).start()

    def x_sent(s):
        for j in range(2):
            for b in range(2):
                px, src, dst, k = x_half(s, j, b)

                @pl.when(jnp.logical_not(x_self(px, b)))
                def _():
                    remote(src, dst, xs.at[s, k], xr.at[s, x], dev(px, y, b, z)).wait_send()

    def x_arrived(s):
        for i in range(NX):
            remote(
                pbuf.at[s, pl.ds(0, 64)], rbuf.at[s, i], xs.at[s, 0], xr.at[s, i], sibling
            ).wait_recv()

    def y_copy(s):
        return remote(
            sbuf.at[s], ybuf.at[s], ys.at[s], yr.at[s], row_dev[s]
        )

    def piece(py_hi, px, pcore):
        at = (py_hi * (2 * NX) + px * 2 + pcore) * 64
        return fresh.at[pl.ds(pl.multiple_of(at, 64), 64)]

    partner = dev(x, lax.rem(y + NF, NY), core, z)

    def fresh_copy(i, src, target):
        return remote(src, src, fs.at[i], fr.at[i], target)

    barrier = pltpu.get_barrier_semaphore()
    peers = [sibling, z_next, z_prev]
    for i in range(1, NY):
        peers.append(dev(x, lax.rem(y + i, NY), core, z))
    for i in range(1, NX):
        for b in range(2):
            peers.append(dev(lax.rem(x + i, NX), y, b, z))
    for peer in peers:
        pl.semaphore_signal(
            barrier, inc=1, device_id=peer, device_id_type=pl.DeviceIdType.MESH
        )
    for s in range(CHUNKS):
        own_chunk(s).start()
    for copy in own_state:
        copy.start()
    attn_local.start()
    for i in range(2):
        weight_local(i).start()
    pl.semaphore_wait(barrier, len(peers))

    for s in range(CHUNKS):
        core_chunk(s, core).start()
    attn_remote = remote(attn, abuf.at[core], asend.at[0], arecv.at[0], sibling)
    attn_remote.start()
    for i in range(2):
        weight_to_prev(i).start()
        weight_to_next(1 - i).start()
    acc[...] = jnp.zeros_like(acc)
    for i in range(2):
        weight_local(i).wait()

    def forward(s, h):
        if h == 0:
            own_chunk(s).wait()
            core_chunk(s, 1 - core).wait_recv()
        for d in range(2):

            def go():
                if h > 0:
                    z_arrived(d, s, h - 1).wait_recv()
                z_copy(d, s, h).start()

            if h < 5 or s % 2 == d:
                go()

    def gathered(s):
        z_arrived(s % 2, s, 5).wait_recv()
        z_arrived(1 - s % 2, s, 4).wait_recv()

    def weight_gradient(s):
        gathered(s)
        g = gbuf[s].reshape(2 * group, half)
        a = abuf[...].reshape(2 * group, abuf.shape[-1])
        part = lax.dot_general(g, a, (((0,), (0,)), ((), ())), preferred_element_type=F32)
        pbuf[s] = part.astype(BF16)
        x_start(s)

    def input_gradient(s):
        g = gbuf[s].reshape(2 * group, half)
        acc[...] += jnp.dot(g, wbuf[row_of[s]], preferred_element_type=F32)

    def row_sum(s):
        x_arrived(s)
        total = rbuf[s, 0].astype(F32)
        for i in range(1, NX):
            total = total + rbuf[s, i].astype(F32)
        return total

    def to_owner(s):
        sbuf[s] = row_sum(s).astype(BF16)
        y_copy(s).start()

    def pass_weights():
        remote(wbuf.at[f_up], wbuf.at[f_up], ws.at[0], wr.at[0], y_prev).wait_recv()
        weight_pass_prev().start()
        down = wbuf.at[f_down + NF]
        remote(down, down, ws.at[3], wr.at[3], y_next).wait_recv()
        weight_pass_next().start()

    def weights_here():
        far = lax.rem(f + 2, NF)
        for role, at, source in (
            (1, f_up + NF, y_prev),
            (2, f_down, y_next),
            (4, far, y_prev),
            (5, far + NF, y_next),
        ):
            ref = wbuf.at[at]
            remote(ref, ref, ws.at[role], wr.at[role], source).wait_recv()

    def attn_here():
        attn_local.wait()
        remote(attn, abuf.at[1 - core], asend.at[0], arecv.at[0], sibling).wait_recv()

    def of_slot(k, go):
        for s in range(CHUNKS):
            if STARTS[s] == k:
                go(s)

    for u in range(STARTS[-1] + 7):
        for h in range(5, 3, -1):
            of_slot(u - h, lambda s: forward(s, h))
        if u == 3:
            pass_weights()
        if u == 6:
            attn_here()
        of_slot(u - 6, weight_gradient)
        for h in range(3, -1, -1):
            of_slot(u - h, lambda s: forward(s, h))
        if u == 6:
            weights_here()
        of_slot(u - 7, to_owner)
        of_slot(u - 6, input_gradient)

    gi_copy = remote(acc.at[pl.ds((1 - core) * group, group)], gibuf, gs.at[0], gr.at[0], sibling)
    gi_copy.start()

    summed = row_sum(CHUNKS - 1)
    for s in range(CHUNKS - 1):
        y_copy(s).wait_recv()
        summed = summed + ybuf[s].astype(F32)
    for copy in own_state:
        copy.wait()
    gradient = summed * scale
    moment_next = 0.9 * mom[...] + 0.1 * gradient
    second_next = 0.95 * sec[...] + 0.05 * gradient * gradient
    adam_step = (
        moment_next / (1.0 - 0.9**10) / (jnp.sqrt(second_next / (1.0 - 0.95**10)) + 1e-08)
    )
    master_next = mst[...] - 0.02 * (adam_step + 0.1 * mst[...])
    mine = piece(yh, x, core)
    mine[...] = master_next.astype(BF16)

    sent = []

    def send(i, ref, target):
        copy = fresh_copy(i, ref, target)
        copy.start()
        sent.append(copy)

    def x_peer(i):
        return dev(lax.rem(x + i, NX), y, core, z)

    send(0, mine, partner)
    for i in (2, 1, 3):
        send(i, mine, x_peer(i))
    send(4, mine, sibling)
    moment_new[...] = moment_next
    second_new[...] = second_next
    master_new[...] = master_next

    def sent_chunk(s):
        core_chunk(s, core).wait_send()
        for d in range(2):
            for h in range(6 if s % 2 == d else 5):
                z_copy(d, s, h).wait_send()

        x_sent(s)

        if s < CHUNKS - 1:
            y_copy(s).wait_send()

    for s in range(CHUNKS):
        sent_chunk(s)
    attn_remote.wait_send()
    for i in range(2):
        weight_to_prev(i).wait_send()
        weight_to_next(i).wait_send()
    weight_pass_prev().wait_send()
    weight_pass_next().wait_send()

    far = piece(1 - yh, x, core)
    fresh_copy(0, far, sibling).wait_recv()
    for i in (2, 1, 3):
        send(4 + i, far, x_peer(i))
    send(8, far, sibling)
    gi_copy.wait_recv()
    mine_rows = pl.ds(pl.multiple_of(core * group, group), group)
    gi_out[...] = (acc[mine_rows] + gibuf[...]).astype(BF16)
    for hi, base in ((yh, 0), (1 - yh, 4)):
        for i in (1, 3, 2):
            got = piece(hi, lax.rem(x - i + NX, NX), core)
            fresh_copy(base + i, got, sibling).wait_recv()
            send(8 + base + i if base == 0 else 8 + 3 + i, got, sibling)
    other = 1 - core
    fresh_copy(4, piece(yh, x, other), sibling).wait_recv()
    fresh_copy(8, piece(1 - yh, x, other), sibling).wait_recv()
    for hi, base in ((yh, 8), (1 - yh, 11)):
        for i in (1, 3, 2):
            got = piece(hi, lax.rem(x - i + NX, NX), other)
            fresh_copy(base + i, got, sibling).wait_recv()

    gi_copy.wait_send()
    for copy in sent:
        copy.wait_send()


def settle(*refs):
    n = (len(refs) - 2) // 3
    given, results, held = refs[:n], refs[n : 2 * n], refs[2 * n : 3 * n]
    into, out = refs[-2], refs[-1]
    reads = [pltpu.make_async_copy(given[i], held[i], into.at[i]) for i in range(n)]
    writes = [pltpu.make_async_copy(held[i], results[i], out.at[i]) for i in range(n)]
    for copy in reads:
        copy.start()
    for read, write in zip(reads, writes):
        read.wait()
        write.start()
    for copy in writes:
        copy.wait()


def shards(attn_out, grad_out, weight, master, moment, second):
    nz = lax.axis_size("tensor")
    rows, dout = grad_out.shape
    group, hid = attn_out.shape
    half = dout // (2 * CHUNKS)
    state_rows = master.shape[0]
    total_tokens = rows * lax.axis_size("cuts") * lax.axis_size("fsdp") * nz
    dma = pltpu.SemaphoreType.DMA
    any_spec = pl.BlockSpec(memory_space=pl.ANY)
    vmem_spec = pl.BlockSpec(memory_space=pltpu.VMEM)
    state = jax.ShapeDtypeStruct(master.shape, F32)
    results = pl.pallas_call(
        functools.partial(kernel, nz, 1.0 / math.sqrt(total_tokens)),
        out_shape=(
            jax.ShapeDtypeStruct((group, hid), BF16),
            jax.ShapeDtypeStruct(weight.shape, BF16),
            state,
            state,
            state,
        ),
        in_specs=[any_spec] * 6,
        out_specs=(vmem_spec,) * 5,
        scratch_shapes=[
            pltpu.VMEM((CHUNKS, 2, nz, rows, half), BF16),
            pltpu.VMEM((2, group, hid), BF16),
            pltpu.VMEM((CHUNKS, half, hid), BF16),
            pltpu.VMEM((CHUNKS, half, hid), BF16),
            pltpu.VMEM((CHUNKS, NX, state_rows, hid), BF16),
            pltpu.VMEM((CHUNKS, state_rows, hid), BF16),
            pltpu.VMEM((CHUNKS, state_rows, hid), BF16),
            pltpu.VMEM((2 * group, hid), F32),
            pltpu.VMEM((group, hid), F32),
            pltpu.VMEM((state_rows, hid), F32),
            pltpu.VMEM((state_rows, hid), F32),
            pltpu.VMEM((state_rows, hid), F32),
            dma((2, CHUNKS, 6)),
            dma((2, CHUNKS, 6)),
            dma((CHUNKS,)),
            dma((CHUNKS,)),
            dma((CHUNKS,)),
            dma((1,)),
            dma((1,)),
            dma((1,)),
            dma((6,)),
            dma((6,)),
            dma((2,)),
            dma((CHUNKS, 4)),
            dma((CHUNKS, NX)),
            dma((CHUNKS,)),
            dma((CHUNKS,)),
            dma((16,)),
            dma((16,)),
            dma((1,)),
            dma((1,)),
            dma((3,)),
        ],
        compiler_params=pltpu.CompilerParams(
            collective_id=0, has_side_effects=True, vmem_limit_bytes=VMEM_LIMIT
        ),
    )(attn_out, grad_out, weight, master, moment, second)
    return pl.pallas_call(
        settle,
        out_shape=tuple(jax.ShapeDtypeStruct(r.shape, r.dtype) for r in results),
        in_specs=[any_spec] * len(results),
        out_specs=(any_spec,) * len(results),
        scratch_shapes=[pltpu.VMEM(r.shape, r.dtype) for r in results]
        + [dma((len(results),)), dma((len(results),))],
        compiler_params=pltpu.CompilerParams(vmem_limit_bytes=VMEM_LIMIT),
    )(*results)


def solution(mesh):
    return jax.shard_map(
        shards,
        mesh=mesh,
        in_specs=(
            P(("cuts", "fsdp"), "tensor"),
            P(("cuts", "fsdp", "tensor"), None),
            P("fsdp", "tensor"),
            P(("fsdp", "cuts"), "tensor"),
            P(("fsdp", "cuts"), "tensor"),
            P(("fsdp", "cuts"), "tensor"),
        ),
        out_specs=(
            P(("cuts", "fsdp"), "tensor"),
            P("fsdp", "tensor"),
            P(("fsdp", "cuts"), "tensor"),
            P(("fsdp", "cuts"), "tensor"),
            P(("fsdp", "cuts"), "tensor"),
        ),
        check_vma=False,
    )
```

```python
import functools
import math

import jax
import jax.numpy as jnp
from jax import lax
from jax.experimental import pallas as pl
from jax.experimental.pallas import tpu as pltpu
from jax.sharding import PartitionSpec as P

BF16 = jnp.bfloat16
F32 = jnp.float32
NX, NY, NF = 4, 8, 4
CHUNKS = NY
STARTS = (0, 0, 1, 1, 2, 3, 4, 5)
VMEM_LIMIT = 60 * 1024 * 1024


def kernel(
    nz,
    scale,
    attn,
    gout,
    weight,
    master,
    moment,
    second,
    gi_out,
    fresh_out,
    master_out,
    moment_out,
    second_out,
    gi,
    fresh,
    master_new,
    moment_new,
    second_new,
    gbuf,
    abuf,
    wbuf,
    pbuf,
    rbuf,
    sbuf,
    ybuf,
    acc,
    gibuf,
    mst,
    mom,
    sec,
    zs,
    zr,
    cs,
    cr,
    cl,
    asend,
    arecv,
    aloc,
    ws,
    wr,
    wl,
    xs,
    xr,
    ys,
    yr,
    fs,
    fr,
    gs,
    gr,
    ol,
    outs,
):
    cuts = lax.axis_index("cuts")
    f = lax.axis_index("fsdp")
    z = lax.axis_index("tensor")
    core = lax.rem(cuts, 2)
    x = lax.rem(lax.div(cuts, 2), NX)
    yh = lax.div(cuts, 2 * NX)
    y = yh * NF + f
    rows = gout.shape[0]
    half = 256
    group = rows * nz

    def dev(px, py, pcore, pz):
        return {
            "cuts": lax.div(py, NF) * (2 * NX) + px * 2 + pcore,
            "fsdp": lax.rem(py, NF),
            "tensor": pz,
        }

    def remote(src, dst, send, recv, target):
        return pltpu.make_async_remote_copy(
            src_ref=src,
            dst_ref=dst,
            send_sem=send,
            recv_sem=recv,
            device_id=target,
            device_id_type=pl.DeviceIdType.MESH,
        )

    sibling = dev(x, y, 1 - core, z)
    z_next = dev(x, y, core, lax.rem(z + 1, nz))
    z_prev = dev(x, y, core, lax.rem(z + nz - 1, nz))
    y_next = dev(x, lax.rem(y + 1, NY), core, z)
    y_prev = dev(x, lax.rem(y + NY - 1, NY), core, z)

    own_state = [
        pltpu.make_async_copy(src, dst, ol.at[i])
        for i, (src, dst) in enumerate(((master, mst), (moment, mom), (second, sec)))
    ]
    attn_local = pltpu.make_async_copy(attn, abuf.at[core], aloc.at[0])

    row_of = [lax.rem(y + NF + (1 - 2 * (s % 2)) * ((s + 1) // 2), NY) for s in range(CHUNKS)]
    row_dev = [dev(x, row, core, z) for row in row_of]
    z_of = [lax.rem(z + i, nz) for i in range(nz)]

    def columns(s, of_core):
        to = row_of[s]
        q = lax.rem(to, NF) * 2 + lax.div(to, NF)
        return pl.ds(pl.multiple_of(q * 512 + of_core * half, half), half)

    def own_chunk(s):
        return pltpu.make_async_copy(
            gout.at[:, columns(s, core)], gbuf.at[s, core, z], cl.at[s]
        )

    def core_chunk(s, me):
        return remote(
            gout.at[:, columns(s, 1 - me)], gbuf.at[s, me, z], cs.at[s], cr.at[s], sibling
        )

    def weight_rows(i):
        return pl.ds(pl.multiple_of(i * 512 + core * half, half), half)

    def weight_local(i):
        return pltpu.make_async_copy(
            weight.at[weight_rows(i)], wbuf.at[f + NF * i], wl.at[i]
        )

    f_up, f_down = lax.rem(f + 1, NF), lax.rem(f + NF - 1, NF)

    def weight_to_prev(i):
        return remote(
            weight.at[weight_rows(i)], wbuf.at[f + NF * i], ws.at[i], wr.at[i], y_prev
        )

    def weight_to_next(i):
        return remote(
            weight.at[weight_rows(i)], wbuf.at[f + NF * i], ws.at[2 + i], wr.at[2 + i], y_next
        )

    def weight_pass_prev():
        return remote(wbuf.at[f_up], wbuf.at[f_up], ws.at[4], wr.at[4], y_prev)

    def weight_pass_next():
        return remote(wbuf.at[f_down + NF], wbuf.at[f_down + NF], ws.at[5], wr.at[5], y_next)

    def z_copy(d, s, h):
        if d == 0:
            block = z_of[-h % nz]
            target = z_next
        else:
            block = z_of[h]
            target = z_prev
        ref = gbuf.at[s, :, block]
        return remote(ref, ref, zs.at[d, s, h], zr.at[d, s, h], target)

    def z_first(d, s, same, me):
        of_core = me if same else 1 - me
        pz = z_of[1] if d == 0 else z_of[nz - 1]
        return remote(
            gout.at[:, columns(s, of_core)],
            gbuf.at[s, me, z],
            zs.at[d, s, 0 if same else 6],
            zr.at[d, s, 0 if same else 6],
            dev(x, y, of_core, pz),
        )

    def z_arrived(d, s, h):
        if d == 0:
            block = z_of[(-1 - h) % nz]
            target = z_next
        else:
            block = z_of[1 + h]
            target = z_prev
        ref = gbuf.at[s, :, block]
        return remote(ref, ref, zs.at[d, s, h], zr.at[d, s, h], target)

    def x_half(s, j, b):
        px = 2 * core + j
        src = pbuf.at[s, pl.ds(j * 128 + b * 64, 64)]
        return px, src, rbuf.at[s, x], j * 2 + b

    def x_self(px, b):
        return jnp.logical_and(px == x, core == b)

    def x_start(s):
        for j in range(2):
            for b in range(2):
                px, src, dst, k = x_half(s, j, b)
                here = x_self(px, b)

                @pl.when(here)
                def _():
                    pltpu.make_async_copy(src, dst, xr.at[s, x]).start()

                @pl.when(jnp.logical_not(here))
                def _():
                    remote(src, dst, xs.at[s, k], xr.at[s, x], dev(px, y, b, z)).start()

    def x_sent(s):
        for j in range(2):
            for b in range(2):
                px, src, dst, k = x_half(s, j, b)

                @pl.when(jnp.logical_not(x_self(px, b)))
                def _():
                    remote(src, dst, xs.at[s, k], xr.at[s, x], dev(px, y, b, z)).wait_send()

    def x_arrived(s):
        for i in range(NX):
            remote(
                pbuf.at[s, pl.ds(0, 64)], rbuf.at[s, i], xs.at[s, 0], xr.at[s, i], sibling
            ).wait_recv()

    def y_copy(s):
        return remote(
            sbuf.at[s], ybuf.at[s], ys.at[s], yr.at[s], row_dev[s]
        )

    def piece(py_hi, px, pcore):
        at = (py_hi * (2 * NX) + px * 2 + pcore) * 64
        return fresh.at[pl.ds(pl.multiple_of(at, 64), 64)]

    partner = dev(x, lax.rem(y + NF, NY), core, z)

    def fresh_copy(i, src, target):
        return remote(src, src, fs.at[i], fr.at[i], target)

    barrier = pltpu.get_barrier_semaphore()
    peers = [sibling, z_next, z_prev]
    for pz in (z_of[1], z_of[nz - 1]):
        peers.append(dev(x, y, 1 - core, pz))
    for i in range(1, NY):
        peers.append(dev(x, lax.rem(y + i, NY), core, z))
    for i in range(1, NX):
        for b in range(2):
            peers.append(dev(lax.rem(x + i, NX), y, b, z))
    for peer in peers:
        pl.semaphore_signal(
            barrier, inc=1, device_id=peer, device_id_type=pl.DeviceIdType.MESH
        )
    for s in range(CHUNKS):
        own_chunk(s).start()
    for copy in own_state:
        copy.start()
    attn_local.start()
    for i in range(2):
        weight_local(i).start()
    pl.semaphore_wait(barrier, len(peers))

    attn_remote = remote(attn, abuf.at[core], asend.at[0], arecv.at[0], sibling)
    attn_remote.start()
    for i in range(2):
        weight_to_prev(i).start()
        weight_to_next(1 - i).start()
    acc[...] = jnp.zeros_like(acc)
    for i in range(2):
        weight_local(i).wait()

    def forward(s, h):
        for d in range(2):

            def go():
                if h == 0:
                    for same in (True, False):
                        z_first(d, s, same, core).start()
                    return
                if h == 1:
                    z_first(d, s, True, core).wait_recv()
                    z_first(d, s, False, 1 - core).wait_recv()
                else:
                    z_arrived(d, s, h - 1).wait_recv()
                z_copy(d, s, h).start()

            if h < 5 or s % 2 == d:
                go()

    def gathered(s):
        own_chunk(s).wait()
        core_chunk(s, 1 - core).wait_recv()
        z_arrived(s % 2, s, 5).wait_recv()
        z_arrived(1 - s % 2, s, 4).wait_recv()

    def weight_gradient(s):
        gathered(s)
        g = gbuf[s].reshape(2 * group, half)
        a = abuf[...].reshape(2 * group, abuf.shape[-1])
        part = lax.dot_general(g, a, (((0,), (0,)), ((), ())), preferred_element_type=F32)
        pbuf[s] = part.astype(BF16)
        x_start(s)

    def input_gradient(s):
        g = gbuf[s].reshape(2 * group, half)
        acc[...] += jnp.dot(g, wbuf[row_of[s]], preferred_element_type=F32)

    def row_sum(s):
        x_arrived(s)
        total = rbuf[s, 0].astype(F32)
        for i in range(1, NX):
            total = total + rbuf[s, i].astype(F32)
        return total

    def to_owner(s):
        sbuf[s] = row_sum(s).astype(BF16)
        y_copy(s).start()

    def pass_weights():
        remote(wbuf.at[f_up], wbuf.at[f_up], ws.at[0], wr.at[0], y_prev).wait_recv()
        weight_pass_prev().start()
        down = wbuf.at[f_down + NF]
        remote(down, down, ws.at[3], wr.at[3], y_next).wait_recv()
        weight_pass_next().start()

    def weights_here():
        far = lax.rem(f + 2, NF)
        for role, at, source in (
            (1, f_up + NF, y_prev),
            (2, f_down, y_next),
            (4, far, y_prev),
            (5, far + NF, y_next),
        ):
            ref = wbuf.at[at]
            remote(ref, ref, ws.at[role], wr.at[role], source).wait_recv()

    def attn_here():
        attn_local.wait()
        remote(attn, abuf.at[1 - core], asend.at[0], arecv.at[0], sibling).wait_recv()

    def of_slot(k, go):
        for s in range(CHUNKS):
            if STARTS[s] == k:
                go(s)

    for u in range(STARTS[-1] + 7):
        for h in range(5, 3, -1):
            of_slot(u - h, lambda s: forward(s, h))
        if u == 1:
            for s in range(CHUNKS):
                core_chunk(s, core).start()
        if u == 3:
            pass_weights()
        if u == 6:
            attn_here()
        of_slot(u - 6, weight_gradient)
        for h in range(3, -1, -1):
            of_slot(u - h, lambda s: forward(s, h))
        if u == 6:
            weights_here()
        of_slot(u - 7, to_owner)
        of_slot(u - 6, input_gradient)

    gi_copy = remote(acc.at[pl.ds((1 - core) * group, group)], gibuf, gs.at[0], gr.at[0], sibling)
    gi_copy.start()

    summed = row_sum(CHUNKS - 1)
    for s in range(CHUNKS - 1):
        y_copy(s).wait_recv()
        summed = summed + ybuf[s].astype(F32)
    for copy in own_state:
        copy.wait()
    gradient = summed * scale
    moment_next = 0.9 * mom[...] + 0.1 * gradient
    second_next = 0.95 * sec[...] + 0.05 * gradient * gradient
    adam_step = (
        moment_next / (1.0 - 0.9**10) / (jnp.sqrt(second_next / (1.0 - 0.95**10)) + 1e-08)
    )
    master_next = mst[...] - 0.02 * (adam_step + 0.1 * mst[...])
    mine = piece(yh, x, core)
    mine[...] = master_next.astype(BF16)

    sent = []

    def send(i, ref, target):
        copy = fresh_copy(i, ref, target)
        copy.start()
        sent.append(copy)

    def x_peer(i):
        return dev(lax.rem(x + i, NX), y, core, z)

    send(0, mine, partner)
    for i in (2, 1, 3):
        send(i, mine, x_peer(i))
    send(4, mine, sibling)
    moment_new[...] = moment_next
    second_new[...] = second_next
    master_new[...] = master_next
    written = [
        pltpu.make_async_copy(master_new, master_out, outs.at[0]),
        pltpu.make_async_copy(moment_new, moment_out, outs.at[1]),
        pltpu.make_async_copy(second_new, second_out, outs.at[2]),
    ]
    for copy in written:
        copy.start()

    def sent_chunk(s):
        core_chunk(s, core).wait_send()
        for d in range(2):
            for same in (True, False):
                z_first(d, s, same, core).wait_send()
            for h in range(1, 6 if s % 2 == d else 5):
                z_copy(d, s, h).wait_send()

        x_sent(s)

        if s < CHUNKS - 1:
            y_copy(s).wait_send()

    for s in range(CHUNKS):
        sent_chunk(s)
    attn_remote.wait_send()
    for i in range(2):
        weight_to_prev(i).wait_send()
        weight_to_next(i).wait_send()
    weight_pass_prev().wait_send()
    weight_pass_next().wait_send()

    far = piece(1 - yh, x, core)
    fresh_copy(0, far, sibling).wait_recv()
    for i in (2, 1, 3):
        send(4 + i, far, x_peer(i))
    send(8, far, sibling)
    gi_copy.wait_recv()
    mine_rows = pl.ds(pl.multiple_of(core * group, group), group)
    gi[...] = (acc[mine_rows] + gibuf[...]).astype(BF16)
    written.append(pltpu.make_async_copy(gi, gi_out, outs.at[3]))
    written[-1].start()
    for hi, base in ((yh, 0), (1 - yh, 4)):
        for i in (1, 3, 2):
            got = piece(hi, lax.rem(x - i + NX, NX), core)
            fresh_copy(base + i, got, sibling).wait_recv()
            send(8 + base + i if base == 0 else 8 + 3 + i, got, sibling)
    other = 1 - core
    for n, (hi, own_i, base) in enumerate(((yh, 4, 8), (1 - yh, 8, 11))):
        fresh_copy(own_i, piece(hi, x, other), sibling).wait_recv()
        for i in (1, 3, 2):
            got = piece(hi, lax.rem(x - i + NX, NX), other)
            fresh_copy(base + i, got, sibling).wait_recv()
        size = 2 * NX * 64
        part = pl.ds(pl.multiple_of(hi * size, size), size)
        written.append(pltpu.make_async_copy(fresh.at[part], fresh_out.at[part], outs.at[4 + n]))
        written[-1].start()

    gi_copy.wait_send()
    for copy in sent:
        copy.wait_send()
    for copy in written:
        copy.wait()


def settle(*refs):
    n = (len(refs) - 2) // 3
    given, results, held = refs[:n], refs[n : 2 * n], refs[2 * n : 3 * n]
    into, out = refs[-2], refs[-1]
    reads = [pltpu.make_async_copy(given[i], held[i], into.at[i]) for i in range(n)]
    writes = [pltpu.make_async_copy(held[i], results[i], out.at[i]) for i in range(n)]
    for copy in reads:
        copy.start()
    for read, write in zip(reads, writes):
        read.wait()
        write.start()
    for copy in writes:
        copy.wait()


def shards(attn_out, grad_out, weight, master, moment, second):
    nz = lax.axis_size("tensor")
    rows, dout = grad_out.shape
    group, hid = attn_out.shape
    half = dout // (2 * CHUNKS)
    state_rows = master.shape[0]
    total_tokens = rows * lax.axis_size("cuts") * lax.axis_size("fsdp") * nz
    dma = pltpu.SemaphoreType.DMA
    any_spec = pl.BlockSpec(memory_space=pl.ANY)
    state = jax.ShapeDtypeStruct(master.shape, F32)
    results = pl.pallas_call(
        functools.partial(kernel, nz, 1.0 / math.sqrt(total_tokens)),
        out_shape=(
            jax.ShapeDtypeStruct((group, hid), BF16),
            jax.ShapeDtypeStruct(weight.shape, BF16),
            state,
            state,
            state,
        ),
        in_specs=[any_spec] * 6,
        out_specs=(any_spec,) * 5,
        scratch_shapes=[
            pltpu.VMEM((group, hid), BF16),
            pltpu.VMEM(weight.shape, BF16),
            pltpu.VMEM(master.shape, F32),
            pltpu.VMEM(master.shape, F32),
            pltpu.VMEM(master.shape, F32),
            pltpu.VMEM((CHUNKS, 2, nz, rows, half), BF16),
            pltpu.VMEM((2, group, hid), BF16),
            pltpu.VMEM((CHUNKS, half, hid), BF16),
            pltpu.VMEM((CHUNKS, half, hid), BF16),
            pltpu.VMEM((CHUNKS, NX, state_rows, hid), BF16),
            pltpu.VMEM((CHUNKS, state_rows, hid), BF16),
            pltpu.VMEM((CHUNKS, state_rows, hid), BF16),
            pltpu.VMEM((2 * group, hid), F32),
            pltpu.VMEM((group, hid), F32),
            pltpu.VMEM((state_rows, hid), F32),
            pltpu.VMEM((state_rows, hid), F32),
            pltpu.VMEM((state_rows, hid), F32),
            dma((2, CHUNKS, 7)),
            dma((2, CHUNKS, 7)),
            dma((CHUNKS,)),
            dma((CHUNKS,)),
            dma((CHUNKS,)),
            dma((1,)),
            dma((1,)),
            dma((1,)),
            dma((6,)),
            dma((6,)),
            dma((2,)),
            dma((CHUNKS, 4)),
            dma((CHUNKS, NX)),
            dma((CHUNKS,)),
            dma((CHUNKS,)),
            dma((16,)),
            dma((16,)),
            dma((1,)),
            dma((1,)),
            dma((3,)),
            dma((6,)),
        ],
        compiler_params=pltpu.CompilerParams(
            collective_id=0, has_side_effects=True, vmem_limit_bytes=VMEM_LIMIT
        ),
    )(attn_out, grad_out, weight, master, moment, second)
    return pl.pallas_call(
        settle,
        out_shape=tuple(jax.ShapeDtypeStruct(r.shape, r.dtype) for r in results),
        in_specs=[any_spec] * len(results),
        out_specs=(any_spec,) * len(results),
        scratch_shapes=[pltpu.VMEM(r.shape, r.dtype) for r in results]
        + [dma((len(results),)), dma((len(results),))],
        compiler_params=pltpu.CompilerParams(vmem_limit_bytes=VMEM_LIMIT),
    )(*results)


def solution(mesh):
    return jax.shard_map(
        shards,
        mesh=mesh,
        in_specs=(
            P(("cuts", "fsdp"), "tensor"),
            P(("cuts", "fsdp", "tensor"), None),
            P("fsdp", "tensor"),
            P(("fsdp", "cuts"), "tensor"),
            P(("fsdp", "cuts"), "tensor"),
            P(("fsdp", "cuts"), "tensor"),
        ),
        out_specs=(
            P(("cuts", "fsdp"), "tensor"),
            P("fsdp", "tensor"),
            P(("fsdp", "cuts"), "tensor"),
            P(("fsdp", "cuts"), "tensor"),
            P(("fsdp", "cuts"), "tensor"),
        ),
        check_vma=False,
    )
```

```python
import functools
import math

import jax
import jax.numpy as jnp
from jax import lax
from jax.experimental import pallas as pl
from jax.experimental.pallas import tpu as pltpu
from jax.sharding import PartitionSpec as P

BF16 = jnp.bfloat16
F32 = jnp.float32
NX, NY, NF = 4, 8, 4
CHUNKS = NY
STARTS = (0, 0, 1, 1, 2, 3, 4, 5)
VMEM_LIMIT = 60 * 1024 * 1024


def kernel(
    nz,
    scale,
    attn,
    gout,
    weight,
    master,
    moment,
    second,
    gi_out,
    fresh_out,
    master_out,
    moment_out,
    second_out,
    gi,
    fresh,
    master_new,
    moment_new,
    second_new,
    gbuf,
    abuf,
    wbuf,
    pbuf,
    rbuf,
    sbuf,
    ybuf,
    acc,
    gibuf,
    mst,
    mom,
    sec,
    zs,
    zr,
    cs,
    cr,
    cl,
    asend,
    arecv,
    aloc,
    ws,
    wr,
    wl,
    xs,
    xr,
    ys,
    yr,
    fs,
    fr,
    gs,
    gr,
    ol,
    outs,
):
    cuts = lax.axis_index("cuts")
    f = lax.axis_index("fsdp")
    z = lax.axis_index("tensor")
    core = lax.rem(cuts, 2)
    x = lax.rem(lax.div(cuts, 2), NX)
    yh = lax.div(cuts, 2 * NX)
    y = yh * NF + f
    rows = gout.shape[0]
    half = 256
    group = rows * nz

    def dev(px, py, pcore, pz):
        return {
            "cuts": lax.div(py, NF) * (2 * NX) + px * 2 + pcore,
            "fsdp": lax.rem(py, NF),
            "tensor": pz,
        }

    def remote(src, dst, send, recv, target):
        return pltpu.make_async_remote_copy(
            src_ref=src,
            dst_ref=dst,
            send_sem=send,
            recv_sem=recv,
            device_id=target,
            device_id_type=pl.DeviceIdType.MESH,
        )

    sibling = dev(x, y, 1 - core, z)
    z_next = dev(x, y, core, lax.rem(z + 1, nz))
    z_prev = dev(x, y, core, lax.rem(z + nz - 1, nz))
    y_next = dev(x, lax.rem(y + 1, NY), core, z)
    y_prev = dev(x, lax.rem(y + NY - 1, NY), core, z)

    own_state = [
        pltpu.make_async_copy(src, dst, ol.at[i])
        for i, (src, dst) in enumerate(((master, mst), (moment, mom), (second, sec)))
    ]
    attn_local = pltpu.make_async_copy(attn, abuf.at[core], aloc.at[0])

    row_of = [lax.rem(y + NF + (1 - 2 * (s % 2)) * ((s + 1) // 2), NY) for s in range(CHUNKS)]
    row_dev = [dev(x, row, core, z) for row in row_of]
    z_of = [lax.rem(z + i, nz) for i in range(nz)]

    def columns(s, of_core):
        to = row_of[s]
        q = lax.rem(to, NF) * 2 + lax.div(to, NF)
        return pl.ds(pl.multiple_of(q * 512 + of_core * half, half), half)

    def own_chunk(s):
        return pltpu.make_async_copy(
            gout.at[:, columns(s, core)], gbuf.at[s, core, z], cl.at[s]
        )

    def core_chunk(s, me):
        return remote(
            gout.at[:, columns(s, 1 - me)], gbuf.at[s, me, z], cs.at[s], cr.at[s], sibling
        )

    def weight_rows(i):
        return pl.ds(pl.multiple_of(i * 512 + core * half, half), half)

    def weight_local(i):
        return pltpu.make_async_copy(
            weight.at[weight_rows(i)], wbuf.at[f + NF * i], wl.at[i]
        )

    f_up, f_down = lax.rem(f + 1, NF), lax.rem(f + NF - 1, NF)

    def weight_to_prev(i):
        return remote(
            weight.at[weight_rows(i)], wbuf.at[f + NF * i], ws.at[i], wr.at[i], y_prev
        )

    def weight_to_next(i):
        return remote(
            weight.at[weight_rows(i)], wbuf.at[f + NF * i], ws.at[2 + i], wr.at[2 + i], y_next
        )

    def weight_pass_prev():
        return remote(wbuf.at[f_up], wbuf.at[f_up], ws.at[4], wr.at[4], y_prev)

    def weight_pass_next():
        return remote(wbuf.at[f_down + NF], wbuf.at[f_down + NF], ws.at[5], wr.at[5], y_next)

    def z_copy(d, s, h):
        if d == 0:
            block = z_of[-h % nz]
            target = z_next
        else:
            block = z_of[h]
            target = z_prev
        ref = gbuf.at[s, :, block]
        return remote(ref, ref, zs.at[d, s, h], zr.at[d, s, h], target)

    def z_first(d, s, same, me):
        of_core = me if same else 1 - me
        pz = z_of[1] if d == 0 else z_of[nz - 1]
        return remote(
            gout.at[:, columns(s, of_core)],
            gbuf.at[s, me, z],
            zs.at[d, s, 0 if same else 6],
            zr.at[d, s, 0 if same else 6],
            dev(x, y, of_core, pz),
        )

    def z_arrived(d, s, h):
        if d == 0:
            block = z_of[(-1 - h) % nz]
            target = z_next
        else:
            block = z_of[1 + h]
            target = z_prev
        ref = gbuf.at[s, :, block]
        return remote(ref, ref, zs.at[d, s, h], zr.at[d, s, h], target)

    def x_half(s, j, b):
        px = 2 * core + j
        src = pbuf.at[s, pl.ds(j * 128 + b * 64, 64)]
        return px, src, rbuf.at[s, x], j * 2 + b

    def x_self(px, b):
        return jnp.logical_and(px == x, core == b)

    def x_start(s):
        for j in range(2):
            for b in range(2):
                px, src, dst, k = x_half(s, j, b)
                here = x_self(px, b)

                @pl.when(here)
                def _():
                    pltpu.make_async_copy(src, dst, xr.at[s, x]).start()

                @pl.when(jnp.logical_not(here))
                def _():
                    remote(src, dst, xs.at[s, k], xr.at[s, x], dev(px, y, b, z)).start()

    def x_sent(s):
        for j in range(2):
            for b in range(2):
                px, src, dst, k = x_half(s, j, b)

                @pl.when(jnp.logical_not(x_self(px, b)))
                def _():
                    remote(src, dst, xs.at[s, k], xr.at[s, x], dev(px, y, b, z)).wait_send()

    def x_arrived(s):
        for i in range(NX):
            remote(
                pbuf.at[s, pl.ds(0, 64)], rbuf.at[s, i], xs.at[s, 0], xr.at[s, i], sibling
            ).wait_recv()

    def y_copy(s):
        return remote(
            sbuf.at[s], ybuf.at[s], ys.at[s], yr.at[s], row_dev[s]
        )

    def piece(py_hi, px, pcore):
        at = (py_hi * (2 * NX) + px * 2 + pcore) * 64
        return fresh.at[pl.ds(pl.multiple_of(at, 64), 64)]

    partner = dev(x, lax.rem(y + NF, NY), core, z)

    def fresh_copy(i, src, target):
        return remote(src, src, fs.at[i], fr.at[i], target)

    barrier = pltpu.get_barrier_semaphore()
    peers = [sibling, z_next, z_prev]
    for pz in (z_of[1], z_of[nz - 1]):
        peers.append(dev(x, y, 1 - core, pz))
    for i in range(1, NY):
        peers.append(dev(x, lax.rem(y + i, NY), core, z))
    for i in range(1, NX):
        for b in range(2):
            peers.append(dev(lax.rem(x + i, NX), y, b, z))
    for peer in peers:
        pl.semaphore_signal(
            barrier, inc=1, device_id=peer, device_id_type=pl.DeviceIdType.MESH
        )
    for s in range(CHUNKS):
        own_chunk(s).start()
    for copy in own_state:
        copy.start()
    attn_local.start()
    for i in range(2):
        weight_local(i).start()
    pl.semaphore_wait(barrier, len(peers))

    attn_remote = remote(attn, abuf.at[core], asend.at[0], arecv.at[0], sibling)

    def start_rest():
        for s in range(CHUNKS):
            core_chunk(s, core).start()
        attn_remote.start()
        for i in range(2):
            weight_to_prev(i).start()
            weight_to_next(1 - i).start()
        acc[...] = jnp.zeros_like(acc)
        for i in range(2):
            weight_local(i).wait()

    def forward(s, h):
        for d in range(2):

            def go():
                if h == 0:
                    for same in (True, False):
                        z_first(d, s, same, core).start()
                    return
                if h == 1:
                    z_first(d, s, True, core).wait_recv()
                    z_first(d, s, False, 1 - core).wait_recv()
                else:
                    z_arrived(d, s, h - 1).wait_recv()
                z_copy(d, s, h).start()

            if h < 5 or s % 2 == d:
                go()

    def gathered(s):
        own_chunk(s).wait()
        core_chunk(s, 1 - core).wait_recv()
        z_arrived(s % 2, s, 5).wait_recv()
        z_arrived(1 - s % 2, s, 4).wait_recv()

    def weight_gradient(s):
        gathered(s)
        g = gbuf[s].reshape(2 * group, half)
        a = abuf[...].reshape(2 * group, abuf.shape[-1])
        part = lax.dot_general(g, a, (((0,), (0,)), ((), ())), preferred_element_type=F32)
        pbuf[s] = part.astype(BF16)
        x_start(s)

    def input_gradient(s):
        g = gbuf[s].reshape(2 * group, half)
        acc[...] += jnp.dot(g, wbuf[row_of[s]], preferred_element_type=F32)

    def row_sum(s):
        x_arrived(s)
        total = rbuf[s, 0].astype(F32)
        for i in range(1, NX):
            total = total + rbuf[s, i].astype(F32)
        return total

    def to_owner(s):
        sbuf[s] = row_sum(s).astype(BF16)
        y_copy(s).start()

    def pass_weights():
        remote(wbuf.at[f_up], wbuf.at[f_up], ws.at[0], wr.at[0], y_prev).wait_recv()
        weight_pass_prev().start()
        down = wbuf.at[f_down + NF]
        remote(down, down, ws.at[3], wr.at[3], y_next).wait_recv()
        weight_pass_next().start()

    def weights_here():
        far = lax.rem(f + 2, NF)
        for role, at, source in (
            (1, f_up + NF, y_prev),
            (2, f_down, y_next),
            (4, far, y_prev),
            (5, far + NF, y_next),
        ):
            ref = wbuf.at[at]
            remote(ref, ref, ws.at[role], wr.at[role], source).wait_recv()

    def attn_here():
        attn_local.wait()
        remote(attn, abuf.at[1 - core], asend.at[0], arecv.at[0], sibling).wait_recv()

    def of_slot(k, go):
        for s in range(CHUNKS):
            if STARTS[s] == k:
                go(s)

    for u in range(STARTS[-1] + 7):
        for h in range(5, 3, -1):
            of_slot(u - h, lambda s: forward(s, h))
        if u == 1:
            start_rest()
        if u == 3:
            pass_weights()
        if u == 6:
            attn_here()
        of_slot(u - 6, weight_gradient)
        for h in range(3, -1, -1):
            of_slot(u - h, lambda s: forward(s, h))
        if u == 6:
            weights_here()
        of_slot(u - 7, to_owner)
        of_slot(u - 6, input_gradient)

    gi_copy = remote(acc.at[pl.ds((1 - core) * group, group)], gibuf, gs.at[0], gr.at[0], sibling)
    gi_copy.start()

    summed = row_sum(CHUNKS - 1)
    for s in range(CHUNKS - 1):
        y_copy(s).wait_recv()
        summed = summed + ybuf[s].astype(F32)
    for copy in own_state:
        copy.wait()
    gradient = summed * scale
    moment_next = 0.9 * mom[...] + 0.1 * gradient
    second_next = 0.95 * sec[...] + 0.05 * gradient * gradient
    adam_step = (
        moment_next / (1.0 - 0.9**10) / (jnp.sqrt(second_next / (1.0 - 0.95**10)) + 1e-08)
    )
    master_next = mst[...] - 0.02 * (adam_step + 0.1 * mst[...])
    mine = piece(yh, x, core)
    mine[...] = master_next.astype(BF16)

    sent = []

    def send(i, ref, target):
        copy = fresh_copy(i, ref, target)
        copy.start()
        sent.append(copy)

    def x_peer(i):
        return dev(lax.rem(x + i, NX), y, core, z)

    send(0, mine, partner)
    for i in (2, 1, 3):
        send(i, mine, x_peer(i))
    send(4, mine, sibling)
    moment_new[...] = moment_next
    second_new[...] = second_next
    master_new[...] = master_next
    written = [
        pltpu.make_async_copy(master_new, master_out, outs.at[0]),
        pltpu.make_async_copy(moment_new, moment_out, outs.at[1]),
        pltpu.make_async_copy(second_new, second_out, outs.at[2]),
    ]
    for copy in written:
        copy.start()

    def sent_chunk(s):
        core_chunk(s, core).wait_send()
        for d in range(2):
            for same in (True, False):
                z_first(d, s, same, core).wait_send()
            for h in range(1, 6 if s % 2 == d else 5):
                z_copy(d, s, h).wait_send()

        x_sent(s)

        if s < CHUNKS - 1:
            y_copy(s).wait_send()

    for s in range(CHUNKS):
        sent_chunk(s)
    attn_remote.wait_send()
    for i in range(2):
        weight_to_prev(i).wait_send()
        weight_to_next(i).wait_send()
    weight_pass_prev().wait_send()
    weight_pass_next().wait_send()

    far = piece(1 - yh, x, core)
    fresh_copy(0, far, sibling).wait_recv()
    for i in (2, 1, 3):
        send(4 + i, far, x_peer(i))
    send(8, far, sibling)
    gi_copy.wait_recv()
    mine_rows = pl.ds(pl.multiple_of(core * group, group), group)
    gi[...] = (acc[mine_rows] + gibuf[...]).astype(BF16)
    written.append(pltpu.make_async_copy(gi, gi_out, outs.at[3]))
    written[-1].start()
    for hi, base in ((yh, 0), (1 - yh, 4)):
        for i in (1, 3, 2):
            got = piece(hi, lax.rem(x - i + NX, NX), core)
            fresh_copy(base + i, got, sibling).wait_recv()
            send(8 + base + i if base == 0 else 8 + 3 + i, got, sibling)
    other = 1 - core
    for n, (hi, own_i, base) in enumerate(((yh, 4, 8), (1 - yh, 8, 11))):
        fresh_copy(own_i, piece(hi, x, other), sibling).wait_recv()
        for i in (1, 3, 2):
            got = piece(hi, lax.rem(x - i + NX, NX), other)
            fresh_copy(base + i, got, sibling).wait_recv()
        size = 2 * NX * 64
        part = pl.ds(pl.multiple_of(hi * size, size), size)
        written.append(pltpu.make_async_copy(fresh.at[part], fresh_out.at[part], outs.at[4 + n]))
        written[-1].start()

    gi_copy.wait_send()
    for copy in sent:
        copy.wait_send()
    for copy in written:
        copy.wait()


def settle(*refs):
    n = (len(refs) - 2) // 3
    given, results, held = refs[:n], refs[n : 2 * n], refs[2 * n : 3 * n]
    into, out = refs[-2], refs[-1]
    reads = [pltpu.make_async_copy(given[i], held[i], into.at[i]) for i in range(n)]
    writes = [pltpu.make_async_copy(held[i], results[i], out.at[i]) for i in range(n)]
    for copy in reads:
        copy.start()
    for read, write in zip(reads, writes):
        read.wait()
        write.start()
    for copy in writes:
        copy.wait()


def shards(attn_out, grad_out, weight, master, moment, second):
    nz = lax.axis_size("tensor")
    rows, dout = grad_out.shape
    group, hid = attn_out.shape
    half = dout // (2 * CHUNKS)
    state_rows = master.shape[0]
    total_tokens = rows * lax.axis_size("cuts") * lax.axis_size("fsdp") * nz
    dma = pltpu.SemaphoreType.DMA
    any_spec = pl.BlockSpec(memory_space=pl.ANY)
    state = jax.ShapeDtypeStruct(master.shape, F32)
    results = pl.pallas_call(
        functools.partial(kernel, nz, 1.0 / math.sqrt(total_tokens)),
        out_shape=(
            jax.ShapeDtypeStruct((group, hid), BF16),
            jax.ShapeDtypeStruct(weight.shape, BF16),
            state,
            state,
            state,
        ),
        in_specs=[any_spec] * 6,
        out_specs=(any_spec,) * 5,
        scratch_shapes=[
            pltpu.VMEM((group, hid), BF16),
            pltpu.VMEM(weight.shape, BF16),
            pltpu.VMEM(master.shape, F32),
            pltpu.VMEM(master.shape, F32),
            pltpu.VMEM(master.shape, F32),
            pltpu.VMEM((CHUNKS, 2, nz, rows, half), BF16),
            pltpu.VMEM((2, group, hid), BF16),
            pltpu.VMEM((CHUNKS, half, hid), BF16),
            pltpu.VMEM((CHUNKS, half, hid), BF16),
            pltpu.VMEM((CHUNKS, NX, state_rows, hid), BF16),
            pltpu.VMEM((CHUNKS, state_rows, hid), BF16),
            pltpu.VMEM((CHUNKS, state_rows, hid), BF16),
            pltpu.VMEM((2 * group, hid), F32),
            pltpu.VMEM((group, hid), F32),
            pltpu.VMEM((state_rows, hid), F32),
            pltpu.VMEM((state_rows, hid), F32),
            pltpu.VMEM((state_rows, hid), F32),
            dma((2, CHUNKS, 7)),
            dma((2, CHUNKS, 7)),
            dma((CHUNKS,)),
            dma((CHUNKS,)),
            dma((CHUNKS,)),
            dma((1,)),
            dma((1,)),
            dma((1,)),
            dma((6,)),
            dma((6,)),
            dma((2,)),
            dma((CHUNKS, 4)),
            dma((CHUNKS, NX)),
            dma((CHUNKS,)),
            dma((CHUNKS,)),
            dma((16,)),
            dma((16,)),
            dma((1,)),
            dma((1,)),
            dma((3,)),
            dma((6,)),
        ],
        compiler_params=pltpu.CompilerParams(
            collective_id=0, has_side_effects=True, vmem_limit_bytes=VMEM_LIMIT
        ),
    )(attn_out, grad_out, weight, master, moment, second)
    return pl.pallas_call(
        settle,
        out_shape=tuple(jax.ShapeDtypeStruct(r.shape, r.dtype) for r in results),
        in_specs=[any_spec] * len(results),
        out_specs=(any_spec,) * len(results),
        scratch_shapes=[pltpu.VMEM(r.shape, r.dtype) for r in results]
        + [dma((len(results),)), dma((len(results),))],
        compiler_params=pltpu.CompilerParams(vmem_limit_bytes=VMEM_LIMIT),
    )(*results)


def solution(mesh):
    return jax.shard_map(
        shards,
        mesh=mesh,
        in_specs=(
            P(("cuts", "fsdp"), "tensor"),
            P(("cuts", "fsdp", "tensor"), None),
            P("fsdp", "tensor"),
            P(("fsdp", "cuts"), "tensor"),
            P(("fsdp", "cuts"), "tensor"),
            P(("fsdp", "cuts"), "tensor"),
        ),
        out_specs=(
            P(("cuts", "fsdp"), "tensor"),
            P("fsdp", "tensor"),
            P(("fsdp", "cuts"), "tensor"),
            P(("fsdp", "cuts"), "tensor"),
            P(("fsdp", "cuts"), "tensor"),
        ),
        check_vma=False,
    )
```
